128 devices in a mesh: heads: 4 (over y), seq: 32 (over x, z, core).
Axes of the slice: x: 4, y: 4, z: 4, core: 2. Of those that a mesh axis runs over, the one named last changes fastest.
Arguments:
- inputs: bfloat16 [32768, 2048], P('seq', 'heads'), may hold values from -6 to 6
- w_query: bfloat16 [2048, 2048], P(None, 'heads'), may hold values from -0.125 to 0.125
- w_key: bfloat16 [2048, 2048], P(None, 'heads'), may hold values from -0.125 to 0.125
- w_value: bfloat16 [2048, 2048], P(None, 'heads'), may hold values from -0.125 to 0.125
- w_out: bfloat16 [2048, 2048], P('heads'), may hold values from -0.125 to 0.125
- beta_code: int32 [32768, 16], P('seq', 'heads'), may hold values from 1 to 128, as said below
- gain: float32 [128], replicated, may hold values from 0.5 to 1.5
Outputs:
- mixed: float32 [32768, 2048], P(('seq', 'heads'))
The draws below stay inside these ranges and needn't reach their ends.
Inputs may be any that keep to these rules, and one draw needn't show every extreme that they name: beta_code / 64 lies in (0, 2], the range of the negative-eigenvalue variant of DeltaNet.
All inputs are finite; a program needn't handle non-finite values.
Results may differ from the reference program's by a relative error of at most 0.0034.
Values may be sent and summed in bfloat16 or wider, within the bound.
A program may use at most 128 MiB of HBM per device.

```python
import jax
import jax.numpy as jnp
from jax import lax

H = 16
DK = 128
D = 2048
C = 64
STREAM_ELEMENTS = 32768


def draw_beta_code(key, part):
    category_seed, quick_seed, omission_seed, spike_seed = jax.random.split(key, 4)
    order = jax.random.permutation(category_seed, H)
    slow_heads = order < H // 2
    fast_values = jax.random.randint(quick_seed, (STREAM_ELEMENTS, H), 1, 97)
    dropped = jax.random.randint(omission_seed, (STREAM_ELEMENTS, H), 0, 4) == 0
    lagging_entries = jnp.where(dropped, 127, 128)
    segment_offsets = jax.random.randint(spike_seed, (3,), 0, STREAM_ELEMENTS - 32)
    partition_devices = jnp.arange(STREAM_ELEMENTS)[:, None]
    spike_cluster = jnp.any((partition_devices >= segment_offsets[None, :]) & (partition_devices < segment_offsets[None, :] + 32), axis=1)
    lagging_entries = jnp.where(spike_cluster[:, None], 64, lagging_entries)
    return jnp.where(slow_heads[None, :], lagging_entries, fast_values).astype(jnp.int32)


def level_of(stream_key, dims, cuts, smallest, top_value):
    def one(position, shards_of):
        heights = jax.random.uniform(jax.random.fold_in(jax.random.fold_in(stream_key, 6), position), (shards_of,), jnp.float32, smallest / len(cuts), top_value / len(cuts))
        return jnp.repeat(jnp.exp(heights), dims[position] // shards_of).reshape((-1,) + (1,) * (len(dims) - position - 1))

    level = one(*cuts[0])
    for cut in cuts[1:]:
        level = level * one(*cut)
    return level


def centred(own_key, dims, scale, bound, cuts=(), kind=jnp.bfloat16):
    array = jax.random.normal(own_key, dims, jnp.float32) * scale
    if len(cuts) > 0:
        array = level_of(own_key, dims, cuts, -0.22, 0.18) * array
    return jnp.clip(array, min=-bound, max=bound).astype(kind)


def setup_inputs(seed: int = 0) -> dict:
    key_of = jax.random.split(jax.random.key(seed), 8)
    inputs = centred(key_of[0], (STREAM_ELEMENTS, D), 1.0, 6.0, ((0, 32), (1, 4)))
    w_query = centred(key_of[1], (D, D), D ** -0.5, 0.125, ((1, 4),))
    w_key = centred(key_of[2], (D, D), D ** -0.5, 0.125, ((1, 4),))
    w_value = centred(key_of[3], (D, D), D ** -0.5, 0.125, ((1, 4),))
    w_out = centred(key_of[4], (D, D), D ** -0.5, 0.125, ((0, 4),))
    beta_code = draw_beta_code(jax.random.fold_in(key_of[7], 71), 0)
    gain = jnp.clip(1.0 + 0.1 * jax.random.normal(key_of[6], (DK,), jnp.float32), 0.5, 1.5)
    return {"inputs": inputs, "w_query": w_query, "w_key": w_key, "w_value": w_value, "w_out": w_out, "beta_code": beta_code, "gain": gain}


def unit_norm(field):
    return field * lax.rsqrt(lax.optimization_barrier(jnp.sum(field * field, -1, keepdims=True)) + 1e-06)

def reference(inputs, w_query, w_key, w_value, w_out, beta_code, gain):
    highest_level = lax.Precision.HIGHEST
    query = jnp.dot(inputs.astype(jnp.float32), w_query.astype(jnp.float32), preferred_element_type=jnp.float32).reshape(STREAM_ELEMENTS, H, DK)
    keys = jnp.dot(inputs.astype(jnp.float32), w_key.astype(jnp.float32), preferred_element_type=jnp.float32).reshape(STREAM_ELEMENTS, H, DK)
    values = jnp.dot(inputs.astype(jnp.float32), w_value.astype(jnp.float32), preferred_element_type=jnp.float32).reshape(STREAM_ELEMENTS, H, DK)
    query = unit_norm(query)
    keys = unit_norm(keys)
    strength = beta_code.astype(jnp.float32) / 64.0
    blocks = STREAM_ELEMENTS // C

    def split_point(field):
        return field.reshape(blocks, C, H, DK).transpose(0, 2, 1, 3)
    q_blocks, k_blocks, v_blocks = (split_point(query), split_point(keys), split_point(values))
    b_blocks = strength.reshape(blocks, C, H).transpose(0, 2, 1)
    ident = jnp.eye(C, dtype=jnp.float32)
    strict = jnp.tril(jnp.ones((C, C), jnp.float32), -1)
    inclusive = jnp.tril(jnp.ones((C, C), jnp.float32), 0)

    def advance(running_state, item):
        query_block, key_block, v_b, b_b = item
        inner = jnp.einsum('hik,hjk->hij', key_block, key_block, precision=highest_level)
        lower = ident + strict * (b_b[:, :, None] * inner)
        right = b_b[:, :, None] * jnp.concatenate([key_block, v_b], -1)
        solved = jax.scipy.linalg.solve_triangular(lower, right, lower=True, unit_diagonal=True)
        weight_matrix = solved[..., :DK]
        update_matrix = solved[..., DK:]
        fresh_state = update_matrix - jnp.einsum('znt,ztc->znc', weight_matrix, running_state, precision=highest_level)
        scores = inclusive * jnp.einsum('hik,hjk->hij', query_block, key_block, precision=highest_level)
        layer_result = jnp.einsum('znt,ztc->znc', query_block, running_state, precision=highest_level)
        layer_result = layer_result + jnp.einsum('hij,hjv->hiv', scores, fresh_state, precision=highest_level)
        running_state = running_state + jnp.einsum('pwc,pwq->pcq', key_block, fresh_state, precision=highest_level)
        return (running_state, layer_result)
    start = jnp.zeros((H, DK, DK), jnp.float32)
    _, outputs = lax.scan(advance, start, (q_blocks, k_blocks, v_blocks, b_blocks))
    outputs = outputs.transpose(0, 2, 1, 3).reshape(STREAM_ELEMENTS, H, DK)
    scale = lax.rsqrt(lax.optimization_barrier(jnp.mean(outputs * outputs, -1, keepdims=True)) + 1e-06)
    normed = (outputs * scale * gain).astype(jnp.bfloat16).reshape(STREAM_ELEMENTS, D)
    return jnp.dot(normed.astype(jnp.float32), w_out.astype(jnp.float32), preferred_element_type=jnp.float32)
```

```python
import functools

import jax
import jax.numpy as jnp
from jax import lax
from jax.experimental import pallas as pl
from jax.experimental.pallas import tpu as pltpu
from jax.sharding import PartitionSpec as P

DK = 128
BLOCK = 128
CHUNK = 256
F32 = jnp.float32
BF16 = jnp.bfloat16


def halves(a):
    high = a.astype(BF16)
    return high, (a - high.astype(F32)).astype(BF16)


def dot(a, b):
    return jnp.dot(a, b, preferred_element_type=F32)


def product_narrow(a, b):
    left = jnp.concatenate(halves(a), 1)
    right = jnp.concatenate(halves(b), 1)
    both = dot(left, jnp.concatenate([right, right], 0))
    return both[:, :DK] + both[:, DK:]


def product_wide(a, b):
    a_high, a_low = halves(a)
    b_high, b_low = halves(b)
    first = dot(jnp.concatenate([a_high, a_low], 1), jnp.concatenate([b_high, b_high], 0))
    return first + dot(a_high, b_low)


def unit_norm(field):
    return field * lax.rsqrt(jnp.sum(field * field, -1, keepdims=True) + 1e-06)


def scan_kernel(x_ref, wq_ref, wk_ref, wv_ref, b_ref, state_in, o_ref, state_out):
    parts, rows, depth = x_ref.shape
    groups = wq_ref.shape[1] // DK

    def project(w_ref):
        total = dot(x_ref[0], w_ref[pl.ds(0, depth), :])
        for part in range(1, parts):
            total += dot(x_ref[part], w_ref[pl.ds(part * depth, depth), :])
        return total

    query, keys, values = project(wq_ref), project(wk_ref), project(wv_ref)
    strength = b_ref[...].astype(F32) * (1.0 / 64.0)
    row = lax.broadcasted_iota(jnp.int32, (BLOCK, BLOCK), 0)
    col = lax.broadcasted_iota(jnp.int32, (BLOCK, BLOCK), 1)
    ident = (row == col).astype(F32)
    differ = row ^ col
    level = jnp.zeros((BLOCK, BLOCK), jnp.int32)
    for t in range(1, 7):
        level += (differ >= (1 << t)).astype(jnp.int32)
    level = jnp.where(row > col, level, -1)

    items = [(b, h) for b in range(rows // BLOCK) for h in range(groups)]

    def cut(field, b, h):
        return field[b * BLOCK : (b + 1) * BLOCK, h * DK : (h + 1) * DK]

    q = [unit_norm(cut(query, b, h)) for b, h in items]
    k = [unit_norm(cut(keys, b, h)) for b, h in items]
    beta = [strength[b * BLOCK : (b + 1) * BLOCK, h : h + 1] for b, h in items]
    k_turned = [a.T for a in k]
    grams = [product_narrow(jnp.concatenate([a, c], 0), t) for a, c, t in zip(k, q, k_turned)]
    below = [e * g[:BLOCK] for e, g in zip(beta, grams)]
    scores = [jnp.where(row >= col, g[BLOCK:], 0.0) for g in grams]
    inverse = [ident - jnp.where(level == 0, n, 0.0) for n in below]
    for t in range(1, 7):
        inner = [product_narrow(jnp.where(level == t, n, 0.0), x) for n, x in zip(below, inverse)]
        inverse = [x - product_narrow(x, y) for x, y in zip(inverse, inner)]
    uw = [
        product_wide(x, e * jnp.concatenate([cut(values, b, h), a], 1))
        for x, e, a, (b, h) in zip(inverse, beta, k, items)
    ]
    effect = [product_wide(jnp.concatenate([t, s], 0), m) for t, s, m in zip(k_turned, scores, uw)]
    zero = jnp.zeros((BLOCK, DK), F32)
    state = [state_in[h] for h in range(groups)]
    for (b, h), g, a in zip(items, effect, q):
        step = jnp.concatenate([ident - g[:BLOCK, DK:], a - g[BLOCK:, DK:]], 0)
        after = product_wide(step, state[h])
        state[h] = after[:BLOCK] + jnp.concatenate([g[:BLOCK, :DK], zero], 1)
        o_ref[h, pl.ds(b * BLOCK, BLOCK), :] = after[BLOCK:] + jnp.concatenate(
            [g[BLOCK:, :DK], zero], 1
        )
    for h in range(groups):
        state_out[h] = state[h]


def local_scan(x, w_query, w_key, w_value, beta_code, state):
    parts, rows, depth = x.shape
    width = w_query.shape[1]
    groups = width // DK
    return pl.pallas_call(
        scan_kernel,
        out_shape=[
            jax.ShapeDtypeStruct((groups, rows, 2 * DK), F32),
            jax.ShapeDtypeStruct(state.shape, F32),
        ],
        compiler_params=pltpu.CompilerParams(vmem_limit_bytes=48 * 1024 * 1024),
        cost_estimate=pl.CostEstimate(
            flops=2 * rows * 2048 * width * 6, bytes_accessed=8 << 20, transcendentals=0
        ),
    )(x, w_query, w_key, w_value, beta_code, state)


MESH = pl.DeviceIdType.MESH


def chain_kernel(
    end_ref, o_hbm, gain_ref, out_ref,
    sibling_end, totals, prefixes, row_in, row_out, start_out, start_in, starts, o_ref, parcels,
    pair_send, pair_recv, z_send, z_recv, x_send, x_recv, a_send, a_recv, o_sem,
):
    group = lax.axis_index("heads")
    me = lax.axis_index("seq")
    groups = lax.axis_size("heads")
    core, z, x = me % 2, (me // 2) % 4, me // 8
    sibling = me + 1 - 2 * core

    def at(x, z, core):
        return {"seq": x * 8 + z * 2 + core}

    barrier = pltpu.get_barrier_semaphore()

    def greet(where):
        pl.semaphore_signal(barrier, inc=1, device_id=where, device_id_type=MESH)

    o_copy = pltpu.make_async_copy(o_hbm, o_ref, o_sem)
    o_copy.start()
    greet({"seq": sibling})
    for d in range(1, 4):
        greet(at(x, (z + d) % 4, core))
        greet({"heads": (group + d) % groups})
    greet(at((x + 1) % 4, z, core))
    greet(at((x + 3) % 4, z, core))
    pl.semaphore_wait(barrier, 9)

    mine, theirs = 2 * core, 2 - 2 * core
    pair = pltpu.make_async_remote_copy(
        src_ref=end_ref.at[pl.ds(theirs, 2)], dst_ref=sibling_end,
        send_sem=pair_send.at[0], recv_sem=pair_recv.at[0],
        device_id={"seq": sibling}, device_id_type=MESH,
    )
    pair.start()
    zero = jnp.zeros((DK, DK), F32)
    ident = (
        lax.broadcasted_iota(jnp.int32, (DK, DK), 0) == lax.broadcasted_iota(jnp.int32, (DK, DK), 1)
    ).astype(F32)

    def after(second, first):
        return product_wide(second[:, DK:], first) + jnp.concatenate([second[:, :DK], zero], 1)

    pair.wait()
    early = []
    for i in range(2):
        own, other = end_ref[mine + i], sibling_end[i]
        first = jnp.where(core == 0, own, other)
        second = jnp.where(core == 0, other, own)
        early.append(first)
        totals[z, i] = after(second, first)

    copies = []
    for d in (1, 3, 2):
        copies.append(
            pltpu.make_async_remote_copy(
                src_ref=totals.at[z], dst_ref=totals.at[z],
                send_sem=z_send.at[d - 1], recv_sem=z_recv.at[d - 1],
                device_id=at(x, (z + d) % 4, core), device_id_type=MESH,
            )
        )
        copies[-1].start()

    @pl.when(x == 0)
    def _():
        row_in[...] = jnp.zeros_like(row_in)

    for copy in copies:
        copy.wait()

    low = [after(totals[1, i], totals[0, i]) for i in range(2)]
    high = [after(totals[3, i], totals[2, i]) for i in range(2)]
    whole = [after(b, a) for a, b in zip(low, high)]
    hops = [
        pltpu.make_async_remote_copy(
            src_ref=row_out.at[i], dst_ref=row_in.at[i],
            send_sem=x_send.at[i], recv_sem=x_recv.at[i],
            device_id=at((x + 1) % 4, z, core), device_id_type=MESH,
        )
        for i in range(2)
    ]

    def pass_on(i, state):
        row_out[i] = product_narrow(whole[i][:, DK:], state) + whole[i][:, :DK]
        hops[i].start()

    @pl.when(x == 0)
    def _():
        for i in range(2):
            row_out[i] = whole[i][:, :DK]
            hops[i].start()

    for i in range(2):
        prefixes[0, i] = jnp.concatenate([zero, ident], 1)
        prefixes[1, i] = totals[0, i]
        prefixes[2, i] = low[i]
        prefixes[3, i] = after(totals[2, i], low[i])
    heads = [prefixes[z, i] for i in range(2)]
    seconds = [after(early[i], heads[i]) for i in range(2)]

    for i in range(2):
        @pl.when(x > 0)
        def _():
            hops[i].wait_recv()

        @pl.when(jnp.logical_and(x > 0, x < 3))
        def _():
            pass_on(i, row_in[i])

    for i in range(2):
        both = jnp.concatenate([heads[i], seconds[i]], 0)
        state = product_narrow(both[:, DK:], row_in[i]) + both[:, :DK]
        starts[mine + i] = jnp.where(core == 0, state[:DK], state[DK:])
        start_out[i] = jnp.where(core == 0, state[DK:], state[:DK])
    back = pltpu.make_async_remote_copy(
        src_ref=start_out, dst_ref=start_in,
        send_sem=pair_send.at[1], recv_sem=pair_recv.at[1],
        device_id={"seq": sibling}, device_id_type=MESH,
    )
    back.start()
    o_copy.wait()
    back.wait()
    for i in range(2):
        starts[theirs + i] = start_in[i]

    @pl.when(x < 3)
    def _():
        for i in range(2):
            hops[i].wait_send()

    rows = parcels.shape[1]
    sends = []
    gain = gain_ref[...]
    for d in (1, 2, 3, 0):
        quarter = (group + d) % groups
        for g in range(starts.shape[0]):
            piece = o_ref[g, pl.ds(pl.multiple_of(quarter * rows, rows), rows), :]
            o = piece[:, :DK] + product_narrow(piece[:, DK:], starts[g])
            scale = lax.rsqrt(jnp.mean(o * o, -1, keepdims=True) + 1e-06)
            normed = (o * scale * gain).astype(BF16)
            if d == 0:
                out_ref[group, :, g * DK : (g + 1) * DK] = normed
            else:
                parcels[d - 1, :, g * DK : (g + 1) * DK] = normed
        if d > 0:
            sends.append(
                pltpu.make_async_remote_copy(
                    src_ref=parcels.at[d - 1], dst_ref=out_ref.at[group],
                    send_sem=a_send.at[d - 1], recv_sem=a_recv.at[d - 1],
                    device_id={"heads": quarter}, device_id_type=MESH,
                )
            )
            sends[-1].start()
    for copy in sends:
        copy.wait()


def chain(end, o, gain):
    groups, tokens, _ = o.shape
    shares = lax.axis_size("heads")
    rows = tokens // shares
    dma = pltpu.SemaphoreType.DMA
    vmem = pl.BlockSpec(memory_space=pltpu.VMEM)
    return pl.pallas_call(
        chain_kernel,
        out_shape=jax.ShapeDtypeStruct((shares, rows, groups * DK), BF16),
        in_specs=[vmem, pl.BlockSpec(memory_space=pl.ANY), vmem],
        out_specs=vmem,
        scratch_shapes=[
            pltpu.VMEM((2, DK, 2 * DK), F32),
            pltpu.VMEM((4, 2, DK, 2 * DK), F32),
            pltpu.VMEM((4, 2, DK, 2 * DK), F32),
            pltpu.VMEM((2, DK, DK), F32),
            pltpu.VMEM((2, DK, DK), F32),
            pltpu.VMEM((2, DK, DK), F32),
            pltpu.VMEM((2, DK, DK), F32),
            pltpu.VMEM((groups, DK, DK), F32),
            pltpu.VMEM(o.shape, F32),
            pltpu.VMEM((shares - 1, rows, groups * DK), BF16),
            dma((2,)), dma((2,)), dma((3,)), dma((3,)), dma((2,)), dma((2,)), dma((3,)), dma((3,)),
            dma,
        ],
        compiler_params=pltpu.CompilerParams(
            collective_id=0, has_side_effects=True, vmem_limit_bytes=32 * 1024 * 1024
        ),
        cost_estimate=pl.CostEstimate(flops=10**9, bytes_accessed=64 << 20, transcendentals=0),
    )(end, o, gain)


def out_kernel(y_ref, w_ref, out_ref):
    part = dot(y_ref[0], w_ref[0])

    @pl.when(pl.program_id(0) == 0)
    def _():
        out_ref[...] = part

    @pl.when(pl.program_id(0) > 0)
    def _():
        out_ref[...] += part


def project_out(normed, w_out):
    shares, rows, width = normed.shape
    return pl.pallas_call(
        out_kernel,
        grid=(shares,),
        out_shape=jax.ShapeDtypeStruct((rows, w_out.shape[2]), F32),
        in_specs=[
            pl.BlockSpec((1, rows, width), lambda h: (h, 0, 0)),
            pl.BlockSpec((1, width, w_out.shape[2]), lambda h: (h, 0, 0)),
        ],
        out_specs=pl.BlockSpec((rows, w_out.shape[2]), lambda h: (0, 0)),
        compiler_params=pltpu.CompilerParams(vmem_limit_bytes=32 * 1024 * 1024),
    )(normed, w_out)


def whole_w_out(w_out):
    rows = w_out.shape[0] // lax.axis_size("seq")
    share = lax.dynamic_slice_in_dim(w_out, lax.axis_index("seq") * rows, rows, 0)
    across = lax.all_gather(share, "heads", axis=0, tiled=False)
    return lax.all_gather(across, "seq", axis=1, tiled=False).reshape(
        lax.axis_size("heads"), w_out.shape[0], w_out.shape[1]
    )


def local(inputs, w_query, w_key, w_value, w_out, beta_code, gain):
    tokens = inputs.shape[0]
    groups = w_query.shape[1] // DK
    w_whole = whole_w_out(w_out)
    ident = jnp.broadcast_to(jnp.eye(DK, dtype=F32), (groups, DK, DK))
    state = jnp.concatenate([jnp.zeros((groups, DK, DK), F32), ident], 2)
    outs = []
    for start in range(0, tokens, CHUNK):
        part = slice(start, start + CHUNK)
        piece = lax.all_gather(inputs[part], "heads", axis=0, tiled=False)
        o, state = local_scan(piece, w_query, w_key, w_value, beta_code[part], state)
        outs.append(o)
    normed = chain(state, jnp.concatenate(outs, 1), gain.reshape(1, DK))
    return project_out(normed, w_whole)


def solution(mesh):
    in_specs = (
        P("seq", "heads"),
        P(None, "heads"),
        P(None, "heads"),
        P(None, "heads"),
        P("heads", None),
        P("seq", "heads"),
        P(),
    )
    out_specs = P(("seq", "heads"), None)
    return jax.shard_map(local, mesh=mesh, in_specs=in_specs, out_specs=out_specs, check_vma=False)
```

```python
import functools

import jax
import jax.numpy as jnp
from jax import lax
from jax.experimental import pallas as pl
from jax.experimental.pallas import tpu as pltpu
from jax.sharding import PartitionSpec as P

DK = 128
BLOCK = 128
CHUNK = 256
F32 = jnp.float32
BF16 = jnp.bfloat16


def halves(a):
    high = a.astype(BF16)
    return high, (a - high.astype(F32)).astype(BF16)


def dot(a, b):
    return jnp.dot(a, b, preferred_element_type=F32)


def product_narrow(a, b):
    left = jnp.concatenate(halves(a), 1)
    right = jnp.concatenate(halves(b), 1)
    both = dot(left, jnp.concatenate([right, right], 0))
    return both[:, :DK] + both[:, DK:]


def product_wide(a, b):
    a_high, a_low = halves(a)
    b_high, b_low = halves(b)
    first = dot(jnp.concatenate([a_high, a_low], 1), jnp.concatenate([b_high, b_high], 0))
    return first + dot(a_high, b_low)


def unit_norm(field):
    return field * lax.rsqrt(jnp.sum(field * field, -1, keepdims=True) + 1e-06)


MESH = pl.DeviceIdType.MESH


def iotas():
    return (
        lax.broadcasted_iota(jnp.int32, (BLOCK, BLOCK), 0),
        lax.broadcasted_iota(jnp.int32, (BLOCK, BLOCK), 1),
    )


def scan_chunk(query, keys, values, strength, state_ref, o_ref, start):
    rows, width = query.shape
    groups = width // DK
    row, col = iotas()
    ident = (row == col).astype(F32)
    differ = row ^ col
    level = jnp.zeros((BLOCK, BLOCK), jnp.int32)
    for t in range(1, 7):
        level += (differ >= (1 << t)).astype(jnp.int32)
    level = jnp.where(row > col, level, -1)

    items = [(b, h) for b in range(rows // BLOCK) for h in range(groups)]

    def cut(field, b, h):
        return field[b * BLOCK : (b + 1) * BLOCK, h * DK : (h + 1) * DK]

    q = [unit_norm(cut(query, b, h)) for b, h in items]
    k = [unit_norm(cut(keys, b, h)) for b, h in items]
    beta = [strength[b * BLOCK : (b + 1) * BLOCK, h : h + 1] for b, h in items]
    k_turned = [a.T for a in k]
    grams = [product_narrow(jnp.concatenate([a, c], 0), t) for a, c, t in zip(k, q, k_turned)]
    below = [e * g[:BLOCK] for e, g in zip(beta, grams)]
    scores = [jnp.where(row >= col, g[BLOCK:], 0.0) for g in grams]
    inverse = [ident - jnp.where(level == 0, n, 0.0) for n in below]
    for t in range(1, 7):
        inner = [product_narrow(jnp.where(level == t, n, 0.0), x) for n, x in zip(below, inverse)]
        inverse = [x - product_narrow(x, y) for x, y in zip(inverse, inner)]
    uw = [
        product_wide(x, e * jnp.concatenate([cut(values, b, h), a], 1))
        for x, e, a, (b, h) in zip(inverse, beta, k, items)
    ]
    effect = [product_wide(jnp.concatenate([t, s], 0), m) for t, s, m in zip(k_turned, scores, uw)]
    zero = jnp.zeros((BLOCK, DK), F32)
    state = [state_ref[h] for h in range(groups)]
    for (b, h), g, a in zip(items, effect, q):
        step = jnp.concatenate([ident - g[:BLOCK, DK:], a - g[BLOCK:, DK:]], 0)
        after = product_wide(step, state[h])
        state[h] = after[:BLOCK] + jnp.concatenate([g[:BLOCK, :DK], zero], 1)
        o_ref[h, pl.ds(start + b * BLOCK, BLOCK), :] = after[BLOCK:] + jnp.concatenate(
            [g[BLOCK:, :DK], zero], 1
        )
    for h in range(groups):
        state_ref[h] = state[h]


def layer_kernel(
    x_ref, wq_hbm, wk_hbm, wv_hbm, b_ref, gain_ref, out_ref,
    w_ref, others, end_ref, o_ref,
    sibling_end, totals, row_in, row_out, start_out, start_in, starts, parcels, relays,
    w_sem, g_send, g_recv, f_send, f_recv,
    pair_send, pair_recv, back_send, back_recv, z_send, z_recv, x_send, x_recv,
    a_send, a_recv, r_send, r_recv, p_send, p_recv,
):
    group = lax.axis_index("heads")
    me = lax.axis_index("seq")
    groups = lax.axis_size("heads")
    core, z, x = me % 2, (me // 2) % 4, me // 8
    sibling = me + 1 - 2 * core
    tokens, depth = x_ref.shape
    chunks = tokens // CHUNK
    half = CHUNK // 2

    def at(x, z, core):
        return {"seq": x * 8 + z * 2 + core}

    def beside(d):
        return {"heads": (group + d) % groups}

    def remote(src, dst, send, recv, where):
        return pltpu.make_async_remote_copy(
            src_ref=src, dst_ref=dst, send_sem=send, recv_sem=recv,
            device_id=where, device_id_type=MESH,
        )

    barrier = pltpu.get_barrier_semaphore()

    def greet(where):
        pl.semaphore_signal(barrier, inc=1, device_id=where, device_id_type=MESH)

    greet({"seq": sibling})
    for d in range(1, 4):
        greet(at(x, (z + d) % 4, core))
        greet(beside(d))
    greet(at((x + 1) % 4, z, core))
    greet(at((x + 3) % 4, z, core))
    loads = [
        pltpu.make_async_copy(w, w_ref.at[i], w_sem.at[i])
        for i, w in enumerate((wq_hbm, wk_hbm, wv_hbm))
    ]
    for load in loads:
        load.start()
    pl.semaphore_wait(barrier, 9)

    def direct(c, d):
        rows = pl.ds(pl.multiple_of(c * CHUNK, CHUNK), CHUNK)
        return remote(
            x_ref.at[rows], others.at[d - 1, rows], g_send.at[c, d // 2], g_recv.at[c, d // 2],
            beside(d),
        )

    def onward(c, j):
        rows = pl.ds(pl.multiple_of(c * CHUNK + j * half, half), half)
        return remote(
            others.at[2 * j, rows], others.at[1, rows], f_send.at[c, j], f_recv.at[c, j],
            beside(1 + 2 * j),
        )

    def start_direct(c):
        direct(c, 1).start()
        direct(c, 3).start()

    def start_onward(c):
        direct(c, 1).wait_recv()
        direct(c, 3).wait_recv()
        onward(c, 0).start()
        onward(c, 1).start()

    start_direct(0)
    start_direct(1)
    row, col = iotas()
    ident = (row == col).astype(F32)
    zero = jnp.zeros((DK, DK), F32)
    for h in range(end_ref.shape[0]):
        end_ref[h] = jnp.concatenate([zero, ident], 1)
    start_onward(0)
    start_direct(2)
    for load in loads:
        load.wait()

    def step(c, carry):
        rows = pl.ds(pl.multiple_of(c * CHUNK, CHUNK), CHUNK)

        def part(i, d):
            source = lax.rem(group + groups - d, groups)
            piece = x_ref[rows, :] if d == 0 else others[d - 1, rows, :]
            return dot(piece, w_ref[i, pl.ds(pl.multiple_of(source * depth, depth), depth), :])

        fields = [part(i, 0) + part(i, 1) + part(i, 3) for i in range(3)]
        onward(c, 0).wait_recv()
        onward(c, 1).wait_recv()
        query, keys, values = [f + part(i, 2) for i, f in enumerate(fields)]

        @pl.when(c + 1 < chunks)
        def _():
            start_onward(c + 1)

        @pl.when(c + 3 < chunks)
        def _():
            start_direct(c + 3)

        strength = b_ref[rows, :].astype(F32) * (1.0 / 64.0)
        scan_chunk(
            query, keys, values, strength, end_ref, o_ref, pl.multiple_of(c * CHUNK, CHUNK)
        )
        return carry

    lax.fori_loop(0, chunks, step, 0)

    mine, theirs = 2 * core, 2 - 2 * core

    def after(second, first):
        return product_wide(second[:, DK:], first) + jnp.concatenate([second[:, :DK], zero], 1)

    pairs = [
        remote(
            end_ref.at[theirs + i], sibling_end.at[i], pair_send.at[i], pair_recv.at[i],
            {"seq": sibling},
        )
        for i in range(2)
    ]
    for pair in pairs:
        pair.start()

    @pl.when(x == 0)
    def _():
        row_in[...] = jnp.zeros_like(row_in)

    early = []
    z_copies = []
    for i in range(2):
        pairs[i].wait_recv()
        own, other = end_ref[mine + i], sibling_end[i]
        first = jnp.where(core == 0, own, other)
        second = jnp.where(core == 0, other, own)
        early.append(first)
        totals[i, z] = after(second, first)
        z_copies.append(
            [
                remote(
                    totals.at[i, z], totals.at[i, z], z_send.at[i, d - 1], z_recv.at[i, d - 1],
                    at(x, (z + d) % 4, core),
                )
                for d in (1, 3, 2)
            ]
        )
        for copy in z_copies[i]:
            copy.start()

    hops = [
        remote(
            row_out.at[i], row_in.at[i], x_send.at[i], x_recv.at[i], at((x + 1) % 4, z, core)
        )
        for i in range(2)
    ]

    def pass_on(i, whole):
        @pl.when(x == 0)
        def _():
            row_out[i] = whole[:, :DK]
            hops[i].start()

        @pl.when(jnp.logical_and(x > 0, x < 3))
        def _():
            hops[i].wait_recv()
            row_out[i] = product_narrow(whole[:, DK:], row_in[i]) + whole[:, :DK]
            hops[i].start()

        @pl.when(x == 3)
        def _():
            hops[i].wait_recv()

    def rows_of(i):
        for copy in z_copies[i]:
            copy.wait_recv()
        low = after(totals[i, 1], totals[i, 0])
        high = after(totals[i, 3], totals[i, 2])
        return low, after(high, low)

    def both_cores(i, low):
        none = jnp.concatenate([zero, ident], 1)
        third = after(totals[i, 2], low)
        head = jnp.where(
            z == 0, none, jnp.where(z == 1, totals[i, 0], jnp.where(z == 2, low, third))
        )
        return jnp.concatenate([head, after(early[i], head)], 0)

    quarter_rows = out_ref.shape[2]
    split = quarter_rows // 2
    gain = gain_ref[...]

    def relay(i, j):
        return remote(
            parcels.at[i, 1, pl.ds(j * split, split)], relays.at[i, j],
            r_send.at[i, j], r_recv.at[i, j], beside(1 + 2 * j),
        )

    def relayed(i, j):
        source = (group + 3 - 2 * j) % groups
        return remote(
            relays.at[i, j], out_ref.at[source, i, pl.ds(j * split, split)],
            p_send.at[i, j], p_recv.at[i, j], beside(1 + 2 * j),
        )

    def parcel(i, d):
        return remote(
            parcels.at[i, d - 1], out_ref.at[group, i], a_send.at[i, d // 2], a_recv.at[i, d // 2],
            beside(d),
        )

    backs = [
        remote(
            start_out.at[i], start_in.at[i], back_send.at[i], back_recv.at[i], {"seq": sibling}
        )
        for i in range(2)
    ]

    def states(i, both):
        state = product_narrow(both[:, DK:], row_in[i]) + both[:, :DK]
        start_out[i] = jnp.where(core == 0, state[DK:], state[:DK])
        backs[i].start()
        starts[mine + i] = jnp.where(core == 0, state[:DK], state[DK:])

    def emit(i):
        backs[i].wait_recv()
        starts[theirs + i] = start_in[i]
        for d in (2, 1, 3, 0):
            quarter = (group + d) % groups
            rows = pl.ds(pl.multiple_of(quarter * quarter_rows, quarter_rows), quarter_rows)
            for j in range(2):
                g = i + 2 * j
                piece = o_ref[g, rows, :]
                o = piece[:, :DK] + product_narrow(piece[:, DK:], starts[g])
                scale = lax.rsqrt(jnp.mean(o * o, -1, keepdims=True) + 1e-06)
                normed = (o * scale * gain).astype(BF16)
                if d == 0:
                    out_ref[group, i, :, j * DK : (j + 1) * DK] = normed
                else:
                    parcels[i, d - 1, :, j * DK : (j + 1) * DK] = normed
            if d == 2:
                relay(i, 0).start()
                relay(i, 1).start()
            elif d > 0:
                parcel(i, d).start()

    low0, whole0 = rows_of(0)
    pass_on(0, whole0)
    both0 = both_cores(0, low0)
    low1, whole1 = rows_of(1)
    states(0, both0)
    pass_on(1, whole1)
    both1 = both_cores(1, low1)
    emit(0)
    states(1, both1)
    for j in range(2):
        relay(0, j).wait_recv()
        relayed(0, j).start()
    emit(1)
    for j in range(2):
        relay(1, j).wait_recv()
        relayed(1, j).start()

    for i in range(2):
        for j in range(2):
            parcel(i, 1 + 2 * j).wait_recv()
            relayed(i, j).wait_recv()

    def sent(c, carry):
        for j in range(2):
            direct(c, 1 + 2 * j).wait_send()
            onward(c, j).wait_send()
        return carry

    lax.fori_loop(0, chunks, sent, 0)
    for i in range(2):
        pairs[i].wait_send()
        backs[i].wait_send()
        for copy in z_copies[i]:
            copy.wait_send()
        for j in range(2):
            relay(i, j).wait_send()
            relayed(i, j).wait_send()
            parcel(i, 1 + 2 * j).wait_send()

    @pl.when(x < 3)
    def _():
        for i in range(2):
            hops[i].wait_send()


def layer(x, w_query, w_key, w_value, beta_code, gain):
    tokens, depth = x.shape
    width = w_query.shape[1]
    groups = width // DK
    shares = lax.axis_size("heads")
    rows = tokens // shares
    chunks = tokens // CHUNK
    dma = pltpu.SemaphoreType.DMA
    vmem = pl.BlockSpec(memory_space=pltpu.VMEM)
    anywhere = pl.BlockSpec(memory_space=pl.ANY)
    return pl.pallas_call(
        layer_kernel,
        out_shape=jax.ShapeDtypeStruct((shares, 2, rows, width // 2), BF16),
        in_specs=[vmem, anywhere, anywhere, anywhere, vmem, vmem],
        out_specs=vmem,
        scratch_shapes=[
            pltpu.VMEM((3, shares * depth, width), BF16),
            pltpu.VMEM((shares - 1, tokens, depth), BF16),
            pltpu.VMEM((groups, DK, 2 * DK), F32),
            pltpu.VMEM((groups, tokens, 2 * DK), F32),
            pltpu.VMEM((2, DK, 2 * DK), F32),
            pltpu.VMEM((2, 4, DK, 2 * DK), F32),
            pltpu.VMEM((2, DK, DK), F32),
            pltpu.VMEM((2, DK, DK), F32),
            pltpu.VMEM((2, DK, DK), F32),
            pltpu.VMEM((2, DK, DK), F32),
            pltpu.VMEM((groups, DK, DK), F32),
            pltpu.VMEM((2, shares - 1, rows, width // 2), BF16),
            pltpu.VMEM((2, 2, rows // 2, width // 2), BF16),
            dma((3,)), dma((chunks, 2)), dma((chunks, 2)), dma((chunks, 2)), dma((chunks, 2)),
            dma((2,)), dma((2,)), dma((2,)), dma((2,)), dma((2, 3)), dma((2, 3)), dma((2,)), dma((2,)),
            dma((2, 2)), dma((2, 2)), dma((2, 2)), dma((2, 2)), dma((2, 2)), dma((2, 2)),
        ],
        compiler_params=pltpu.CompilerParams(
            collective_id=0, has_side_effects=True, vmem_limit_bytes=48 * 1024 * 1024
        ),
        cost_estimate=pl.CostEstimate(flops=40 * 10**9, bytes_accessed=64 << 20, transcendentals=0),
    )(x, w_query, w_key, w_value, beta_code, gain)


def out_kernel(y_ref, w_ref, out_ref):
    part = 0.0
    for i in range(2):
        w = jnp.concatenate([w_ref[0, pl.ds(i * DK, DK)], w_ref[0, pl.ds((i + 2) * DK, DK)]], 0)
        part += dot(y_ref[0, i], w)

    @pl.when(pl.program_id(0) == 0)
    def _():
        out_ref[...] = part

    @pl.when(pl.program_id(0) > 0)
    def _():
        out_ref[...] += part


def project_out(normed, w_out):
    shares, parts, rows, width = normed.shape
    return pl.pallas_call(
        out_kernel,
        grid=(shares,),
        out_shape=jax.ShapeDtypeStruct((rows, w_out.shape[2]), F32),
        in_specs=[
            pl.BlockSpec((1, parts, rows, width), lambda h: (h, 0, 0, 0)),
            pl.BlockSpec((1, parts * width, w_out.shape[2]), lambda h: (h, 0, 0)),
        ],
        out_specs=pl.BlockSpec((rows, w_out.shape[2]), lambda h: (0, 0)),
        compiler_params=pltpu.CompilerParams(vmem_limit_bytes=32 * 1024 * 1024),
    )(normed, w_out)


def whole_w_out(w_out):
    rows = w_out.shape[0] // lax.axis_size("seq")
    share = lax.dynamic_slice_in_dim(w_out, lax.axis_index("seq") * rows, rows, 0)
    return lax.all_gather(share, ("heads", "seq"), axis=0, tiled=True).reshape(
        lax.axis_size("heads"), w_out.shape[0], w_out.shape[1]
    )


def local(inputs, w_query, w_key, w_value, w_out, beta_code, gain):
    w_whole = whole_w_out(w_out)
    normed = layer(inputs, w_query, w_key, w_value, beta_code, gain.reshape(1, DK))
    return project_out(normed, w_whole)


def solution(mesh):
    in_specs = (
        P("seq", "heads"),
        P(None, "heads"),
        P(None, "heads"),
        P(None, "heads"),
        P("heads", None),
        P("seq", "heads"),
        P(),
    )
    out_specs = P(("seq", "heads"), None)
    return jax.shard_map(local, mesh=mesh, in_specs=in_specs, out_specs=out_specs, check_vma=False)
```

```python
import functools

import jax
import jax.numpy as jnp
from jax import lax
from jax.experimental import pallas as pl
from jax.experimental.pallas import tpu as pltpu
from jax.sharding import PartitionSpec as P

DK = 128
BLOCK = 128
CHUNK = 256
F32 = jnp.float32
BF16 = jnp.bfloat16


def halves(a):
    high = a.astype(BF16)
    return high, (a - high.astype(F32)).astype(BF16)


def dot(a, b):
    return jnp.dot(a, b, preferred_element_type=F32)


def product_narrow(a, b):
    left = jnp.concatenate(halves(a), 1)
    right = jnp.concatenate(halves(b), 1)
    both = dot(left, jnp.concatenate([right, right], 0))
    return both[:, :DK] + both[:, DK:]


def product_wide(a, b):
    a_high, a_low = halves(a)
    b_high, b_low = halves(b)
    first = dot(jnp.concatenate([a_high, a_low], 1), jnp.concatenate([b_high, b_high], 0))
    return first + dot(a_high, b_low)


def unit_norm(field):
    return field * lax.rsqrt(jnp.sum(field * field, -1, keepdims=True) + 1e-06)


MESH = pl.DeviceIdType.MESH


def iotas():
    return (
        lax.broadcasted_iota(jnp.int32, (BLOCK, BLOCK), 0),
        lax.broadcasted_iota(jnp.int32, (BLOCK, BLOCK), 1),
    )


def scan_chunk(query, keys, values, strength, state_ref, o_ref, start):
    rows, width = query.shape
    groups = width // DK
    row, col = iotas()
    ident = (row == col).astype(F32)
    differ = row ^ col
    level = jnp.zeros((BLOCK, BLOCK), jnp.int32)
    for t in range(1, 7):
        level += (differ >= (1 << t)).astype(jnp.int32)
    level = jnp.where(row > col, level, -1)

    items = [(b, h) for b in range(rows // BLOCK) for h in range(groups)]

    def cut(field, b, h):
        return field[b * BLOCK : (b + 1) * BLOCK, h * DK : (h + 1) * DK]

    q = [unit_norm(cut(query, b, h)) for b, h in items]
    k = [unit_norm(cut(keys, b, h)) for b, h in items]
    beta = [strength[b * BLOCK : (b + 1) * BLOCK, h : h + 1] for b, h in items]
    k_turned = [a.T for a in k]
    grams = [product_narrow(jnp.concatenate([a, c], 0), t) for a, c, t in zip(k, q, k_turned)]
    below = [e * g[:BLOCK] for e, g in zip(beta, grams)]
    scores = [jnp.where(row >= col, g[BLOCK:], 0.0) for g in grams]
    inverse = [ident - jnp.where(level == 0, n, 0.0) for n in below]
    for t in range(1, 7):
        inner = [product_narrow(jnp.where(level == t, n, 0.0), x) for n, x in zip(below, inverse)]
        inverse = [x - product_narrow(x, y) for x, y in zip(inverse, inner)]
    uw = [
        product_wide(x, e * jnp.concatenate([cut(values, b, h), a], 1))
        for x, e, a, (b, h) in zip(inverse, beta, k, items)
    ]
    effect = [product_wide(jnp.concatenate([t, s], 0), m) for t, s, m in zip(k_turned, scores, uw)]
    zero = jnp.zeros((BLOCK, DK), F32)
    state = [state_ref[h] for h in range(groups)]
    for (b, h), g, a in zip(items, effect, q):
        step = jnp.concatenate([ident - g[:BLOCK, DK:], a - g[BLOCK:, DK:]], 0)
        after = product_wide(step, state[h])
        state[h] = after[:BLOCK] + jnp.concatenate([g[:BLOCK, :DK], zero], 1)
        o_ref[h, pl.ds(start + b * BLOCK, BLOCK), :] = after[BLOCK:] + jnp.concatenate(
            [g[BLOCK:, :DK], zero], 1
        )
    for h in range(groups):
        state_ref[h] = state[h]


def layer_kernel(
    x_hbm, wq_hbm, wk_hbm, wv_hbm, wo_hbm, b_hbm, gain_hbm, out_ref,
    x_ref, b_ref, gain_ref, w_ref, wo_ref, others, end_ref, o_ref,
    sibling_end, totals, row_in, row_out, start_out, start_in, starts, parcels, relays, got,
    w_sem, l_sem, g_send, g_recv, f_send, f_recv,
    across_send, across_recv, first_send, first_recv, second_send, second_recv,
    third_send, third_recv, fourth_send, fourth_recv,
    pair_send, pair_recv, back_send, back_recv, z_send, z_recv, x_send, x_recv,
    a_send, a_recv, r_send, r_recv, p_send, p_recv,
):
    group = lax.axis_index("heads")
    me = lax.axis_index("seq")
    groups = lax.axis_size("heads")
    core, z, x = me % 2, (me // 2) % 4, me // 8
    sibling = me + 1 - 2 * core
    tokens, depth = x_ref.shape
    chunks = tokens // CHUNK
    half = CHUNK // 2

    def at(x, z, core):
        return {"seq": x * 8 + z * 2 + core}

    def beside(d):
        return {"heads": (group + d) % groups}

    def remote(src, dst, send, recv, where):
        return pltpu.make_async_remote_copy(
            src_ref=src, dst_ref=dst, send_sem=send, recv_sem=recv,
            device_id=where, device_id_type=MESH,
        )

    barrier = pltpu.get_barrier_semaphore()

    def greet(where):
        pl.semaphore_signal(barrier, inc=1, device_id=where, device_id_type=MESH)

    greet({"seq": sibling})
    for d in range(1, 4):
        greet(at(x, (z + d) % 4, core))
        greet(beside(d))
        greet(at((x + d) % 4, z, core))
    loads = [
        pltpu.make_async_copy(w, w_ref.at[i], w_sem.at[i])
        for i, w in enumerate((wq_hbm, wk_hbm, wv_hbm))
    ]
    for load in loads:
        load.start()
    smalls = [
        pltpu.make_async_copy(x_hbm, x_ref, l_sem.at[0]),
        pltpu.make_async_copy(b_hbm, b_ref, l_sem.at[1]),
        pltpu.make_async_copy(gain_hbm, gain_ref, l_sem.at[2]),
    ]
    for load in smalls:
        load.start()
    pl.semaphore_wait(barrier, 10)

    across = [
        remote(
            wo_hbm.at[x, z, core], wo_ref.at[d, x, z, core],
            across_send.at[d - 1], across_recv.at[d - 1], beside(d),
        )
        for d in (1, 3, 2)
    ]
    back = pl.ds(1, 3)

    def along(core_now, first, d):
        if (core_now == 0) == first:
            return at(x, (z + d) % 4, core)
        return at((x + d) % 4, z, core)

    def firsts(core_now):
        return [
            remote(
                wo_ref.at[back, x, z, core_now], wo_ref.at[back, x, z, core_now],
                first_send.at[d - 1], first_recv.at[d - 1], along(core_now, True, d),
            )
            for d in (1, 3, 2)
        ]

    def line(core_now, place):
        if core_now == 0:
            return wo_ref.at[back, place, :, 0]
        return wo_ref.at[back, :, place, 1]

    def seconds(core_now):
        here = line(core_now, x if core_now == 0 else z)
        return [
            remote(
                here, here, second_send.at[d // 2], second_recv.at[d // 2],
                along(core_now, False, d),
            )
            for d in (1, 3)
        ]

    def half_line(core_now, place, j):
        if core_now == 0:
            return wo_ref.at[back, place, pl.ds(2 * j, 2), 0]
        return wo_ref.at[back, pl.ds(2 * j, 2), place, 1]

    def thirds(core_now):
        place = x if core_now == 0 else z
        return [
            remote(
                half_line(core_now, (place + 3 - 2 * j) % 4, j),
                half_line(core_now, (place + 3 - 2 * j) % 4, j),
                third_send.at[j], third_recv.at[j], along(core_now, False, 1 + 2 * j),
            )
            for j in range(2)
        ]

    def fourth():
        here = wo_ref.at[back, :, :, core]
        return remote(here, here, fourth_send.at[0], fourth_recv.at[0], {"seq": sibling})

    def either(do):
        for core_now in range(2):
            @pl.when(core == core_now)
            def _():
                do(core_now)

    def begin(copies):
        for copy in copies:
            copy.start()

    def arrived(copies):
        for copy in copies:
            copy.wait_recv()

    def left(copies):
        for copy in copies:
            copy.wait_send()

    begin(across)
    own_w = [pltpu.make_async_copy(wo_hbm, wo_ref.at[0], l_sem.at[3])]
    begin(own_w)

    def direct(c, d):
        rows = pl.ds(pl.multiple_of(c * CHUNK, CHUNK), CHUNK)
        return remote(
            x_hbm.at[rows], others.at[d - 1, rows], g_send.at[c, d // 2], g_recv.at[c, d // 2],
            beside(d),
        )

    def onward(c, j):
        rows = pl.ds(pl.multiple_of(c * CHUNK + j * half, half), half)
        return remote(
            others.at[2 * j, rows], others.at[1, rows], f_send.at[c, j], f_recv.at[c, j],
            beside(1 + 2 * j),
        )

    def start_direct(c):
        direct(c, 1).start()
        direct(c, 3).start()

    def start_onward(c):
        direct(c, 1).wait_recv()
        direct(c, 3).wait_recv()
        onward(c, 0).start()
        onward(c, 1).start()

    start_direct(0)
    start_direct(1)
    row, col = iotas()
    ident = (row == col).astype(F32)
    zero = jnp.zeros((DK, DK), F32)
    for h in range(end_ref.shape[0]):
        end_ref[h] = jnp.concatenate([zero, ident], 1)
    arrived(across)
    either(lambda core_now: begin(firsts(core_now)))
    start_onward(0)
    start_direct(2)
    for load in loads + smalls:
        load.wait()

    def step(c, carry):
        rows = pl.ds(pl.multiple_of(c * CHUNK, CHUNK), CHUNK)

        def part(i, d):
            source = lax.rem(group + groups - d, groups)
            piece = x_ref[rows, :] if d == 0 else others[d - 1, rows, :]
            return dot(piece, w_ref[i, pl.ds(pl.multiple_of(source * depth, depth), depth), :])

        fields = [part(i, 0) + part(i, 1) + part(i, 3) for i in range(3)]
        onward(c, 0).wait_recv()
        onward(c, 1).wait_recv()
        query, keys, values = [f + part(i, 2) for i, f in enumerate(fields)]

        @pl.when(c + 1 < chunks)
        def _():
            start_onward(c + 1)

        @pl.when(c + 3 < chunks)
        def _():
            start_direct(c + 3)

        @pl.when(c == 0)
        def _():
            def go(core_now):
                arrived(firsts(core_now))
                begin(seconds(core_now))

            either(go)

        @pl.when(c == 1)
        def _():
            def go(core_now):
                arrived(seconds(core_now))
                begin(thirds(core_now))

            either(go)

        @pl.when(c == 2)
        def _():
            either(lambda core_now: arrived(thirds(core_now)))
            fourth().start()

        strength = (b_ref[:, rows].astype(F32) * (1.0 / 64.0)).T
        scan_chunk(
            query, keys, values, strength, end_ref, o_ref, pl.multiple_of(c * CHUNK, CHUNK)
        )
        return carry

    lax.fori_loop(0, chunks, step, 0)

    mine, theirs = 2 * core, 2 - 2 * core

    def after(second, first):
        return product_wide(second[:, DK:], first) + jnp.concatenate([second[:, :DK], zero], 1)

    pairs = [
        remote(
            end_ref.at[theirs + i], sibling_end.at[i], pair_send.at[i], pair_recv.at[i],
            {"seq": sibling},
        )
        for i in range(2)
    ]
    for pair in pairs:
        pair.start()

    @pl.when(x == 0)
    def _():
        row_in[...] = jnp.zeros_like(row_in)

    early = []
    z_copies = []
    for i in range(2):
        pairs[i].wait_recv()
        own, other = end_ref[mine + i], sibling_end[i]
        first = jnp.where(core == 0, own, other)
        second = jnp.where(core == 0, other, own)
        early.append(first)
        totals[i, z] = after(second, first)
        z_copies.append(
            [
                remote(
                    totals.at[i, z], totals.at[i, z], z_send.at[i, d // 2], z_recv.at[i, d // 2],
                    at(x, (z + d) % 4, core),
                )
                for d in (1, 3)
            ]
        )
        if i == 0:
            begin(z_copies[i])

    hops = [
        remote(
            row_out.at[i], row_in.at[i], x_send.at[i], x_recv.at[i], at((x + 1) % 4, z, core)
        )
        for i in range(2)
    ]

    def set_out(i, whole):
        @pl.when(x == 0)
        def _():
            row_out[i] = whole[:, :DK]
            hops[i].start()

    def pass_on(i, whole):
        @pl.when(jnp.logical_and(x > 0, x < 3))
        def _():
            hops[i].wait_recv()
            row_out[i] = product_narrow(whole[:, DK:], row_in[i]) + whole[:, :DK]
            hops[i].start()

        @pl.when(x == 3)
        def _():
            hops[i].wait_recv()

    def z_onward(i):
        return [
            remote(
                totals.at[i, (z + 3 - 2 * j) % 4, pl.ds(j * (DK // 2), DK // 2)],
                totals.at[i, (z + 3 - 2 * j) % 4, pl.ds(j * (DK // 2), DK // 2)],
                z_send.at[i, 2 + j], z_recv.at[i, 2 + j], at(x, (z + 1 + 2 * j) % 4, core),
            )
            for j in range(2)
        ]

    def rows_of(i):
        arrived(z_onward(i))
        low = after(totals[i, 1], totals[i, 0])
        high = after(totals[i, 3], totals[i, 2])
        return low, after(high, low)

    def both_cores(i, low):
        none = jnp.concatenate([zero, ident], 1)
        third = after(totals[i, 2], low)
        head = jnp.where(
            z == 0, none, jnp.where(z == 1, totals[i, 0], jnp.where(z == 2, low, third))
        )
        return jnp.concatenate([head, after(early[i], head)], 0)

    quarter_rows = got.shape[2]
    split = quarter_rows // 2
    gain = gain_ref[...]

    def relay(i, j):
        return remote(
            parcels.at[i, 1, pl.ds(j * split, split)], relays.at[i, j],
            r_send.at[i, j], r_recv.at[i, j], beside(1 + 2 * j),
        )

    def relayed(i, j):
        return remote(
            relays.at[i, j], got.at[2, i, pl.ds(j * split, split)],
            p_send.at[i, j], p_recv.at[i, j], beside(1 + 2 * j),
        )

    def parcel(i, d):
        return remote(
            parcels.at[i, d - 1], got.at[d, i], a_send.at[i, d // 2], a_recv.at[i, d // 2],
            beside(d),
        )

    backs = [
        remote(
            start_out.at[i], start_in.at[i], back_send.at[i], back_recv.at[i], {"seq": sibling}
        )
        for i in range(2)
    ]

    def states(i, both):
        state = product_narrow(both[:, DK:], row_in[i]) + both[:, :DK]
        start_out[i] = jnp.where(core == 0, state[DK:], state[:DK])
        backs[i].start()
        starts[mine + i] = jnp.where(core == 0, state[:DK], state[DK:])

    def emit(i):
        backs[i].wait_recv()
        starts[theirs + i] = start_in[i]
        for d in (2, 1, 3, 0):
            quarter = (group + d) % groups
            rows = pl.ds(pl.multiple_of(quarter * quarter_rows, quarter_rows), quarter_rows)
            for j in range(2):
                g = i + 2 * j
                piece = o_ref[g, rows, :]
                o = piece[:, :DK] + product_narrow(piece[:, DK:], starts[g])
                scale = lax.rsqrt(jnp.mean(o * o, -1, keepdims=True) + 1e-06)
                normed = (o * scale * gain).astype(BF16)
                if d == 0:
                    got[0, i, :, j * DK : (j + 1) * DK] = normed
                else:
                    parcels[i, d - 1, :, j * DK : (j + 1) * DK] = normed
            if d == 2:
                relay(i, 0).start()
                relay(i, 1).start()
            elif d > 0:
                parcel(i, d).start()

    columns = out_ref.shape[1]
    tile = 512

    def mix(i, d, first=False):
        def one(n, carry):
            lanes = pl.ds(pl.multiple_of(n * tile, tile), tile)
            w = [
                wo_ref[d, i + 2 * j, :, :, :, lanes].reshape(DK, tile)
                for j in range(2)
            ]
            part = dot(got[d, i], jnp.concatenate(w, 0))
            if first:
                out_ref[:, lanes] = part
            else:
                out_ref[:, lanes] += part
            return carry

        lax.fori_loop(0, columns // tile, one, 0)

    arrived(z_copies[0])
    begin(z_onward(0))
    begin(z_copies[1])
    low0, whole0 = rows_of(0)
    set_out(0, whole0)
    both0 = both_cores(0, low0)
    arrived(z_copies[1])
    begin(z_onward(1))
    pass_on(0, whole0)
    states(0, both0)
    low1, whole1 = rows_of(1)
    set_out(1, whole1)
    both1 = both_cores(1, low1)
    emit(0)
    pass_on(1, whole1)
    states(1, both1)
    for j in range(2):
        relay(0, j).wait_recv()
        relayed(0, j).start()
    fourth().wait_recv()
    for load in own_w:
        load.wait()
    mix(0, 0, True)
    emit(1)
    for j in range(2):
        relay(1, j).wait_recv()
        relayed(1, j).start()
    mix(1, 0)
    for i in range(2):
        for d in (1, 3):
            parcel(i, d).wait_recv()
            mix(i, d)
        relayed(i, 0).wait_recv()
        relayed(i, 1).wait_recv()
        mix(i, 2)

    def sent(c, carry):
        for j in range(2):
            direct(c, 1 + 2 * j).wait_send()
            onward(c, j).wait_send()
        return carry

    lax.fori_loop(0, chunks, sent, 0)
    left(across)
    either(lambda core_now: left(firsts(core_now) + seconds(core_now) + thirds(core_now)))
    left([fourth()])
    for i in range(2):
        pairs[i].wait_send()
        backs[i].wait_send()
        left(z_copies[i] + z_onward(i))
        for j in range(2):
            relay(i, j).wait_send()
            relayed(i, j).wait_send()
            parcel(i, 1 + 2 * j).wait_send()

    @pl.when(x < 3)
    def _():
        for i in range(2):
            hops[i].wait_send()


def local(inputs, w_query, w_key, w_value, w_out, beta_code, gain):
    tokens, depth = inputs.shape
    width = w_query.shape[1]
    groups = width // DK
    shares = lax.axis_size("heads")
    shards = lax.axis_size("seq")
    rows = tokens // shares
    chunks = tokens // CHUNK
    columns = w_out.shape[1]
    w_parts = w_out.reshape(4, 4, 2, width // shards, columns)
    dma = pltpu.SemaphoreType.DMA
    anywhere = pl.BlockSpec(memory_space=pl.ANY)
    return pl.pallas_call(
        layer_kernel,
        out_shape=jax.ShapeDtypeStruct((rows, columns), F32),
        in_specs=[anywhere] * 7,
        out_specs=pl.BlockSpec(memory_space=pltpu.VMEM),
        scratch_shapes=[
            pltpu.VMEM((tokens, depth), BF16),
            pltpu.VMEM((groups, tokens), jnp.int32),
            pltpu.VMEM((1, DK), F32),
            pltpu.VMEM((3, shares * depth, width), BF16),
            pltpu.VMEM((shares, 4, 4, 2, width // shards, columns), BF16),
            pltpu.VMEM((shares - 1, tokens, depth), BF16),
            pltpu.VMEM((groups, DK, 2 * DK), F32),
            pltpu.VMEM((groups, tokens, 2 * DK), F32),
            pltpu.VMEM((2, DK, 2 * DK), F32),
            pltpu.VMEM((2, 4, DK, 2 * DK), F32),
            pltpu.VMEM((2, DK, DK), F32),
            pltpu.VMEM((2, DK, DK), F32),
            pltpu.VMEM((2, DK, DK), F32),
            pltpu.VMEM((2, DK, DK), F32),
            pltpu.VMEM((groups, DK, DK), F32),
            pltpu.VMEM((2, shares - 1, rows, width // 2), BF16),
            pltpu.VMEM((2, 2, rows // 2, width // 2), BF16),
            pltpu.VMEM((shares, 2, rows, width // 2), BF16),
            dma((3,)), dma((4,)),
            dma((chunks, 2)), dma((chunks, 2)), dma((chunks, 2)), dma((chunks, 2)),
            dma((3,)), dma((3,)), dma((3,)), dma((3,)), dma((2,)), dma((2,)),
            dma((2,)), dma((2,)), dma((1,)), dma((1,)),
            dma((2,)), dma((2,)), dma((2,)), dma((2,)), dma((2, 4)), dma((2, 4)), dma((2,)), dma((2,)),
            dma((2, 2)), dma((2, 2)), dma((2, 2)), dma((2, 2)), dma((2, 2)), dma((2, 2)),
        ],
        compiler_params=pltpu.CompilerParams(
            collective_id=0, has_side_effects=True, vmem_limit_bytes=60 * 1024 * 1024
        ),
        cost_estimate=pl.CostEstimate(flops=40 * 10**9, bytes_accessed=64 << 20, transcendentals=0),
    )(inputs, w_query, w_key, w_value, w_parts, beta_code.T, gain.reshape(1, DK))


def solution(mesh):
    in_specs = (
        P("seq", "heads"),
        P(None, "heads"),
        P(None, "heads"),
        P(None, "heads"),
        P("heads", None),
        P("seq", "heads"),
        P(),
    )
    out_specs = P(("seq", "heads"), None)
    return jax.shard_map(local, mesh=mesh, in_specs=in_specs, out_specs=out_specs, check_vma=False)
```

```python
import functools

import jax
import jax.numpy as jnp
from jax import lax
from jax.experimental import pallas as pl
from jax.experimental.pallas import tpu as pltpu
from jax.sharding import PartitionSpec as P

DK = 128
BLOCK = 128
CHUNK = 256
F32 = jnp.float32
BF16 = jnp.bfloat16


def halves(a):
    high = a.astype(BF16)
    return high, (a - high.astype(F32)).astype(BF16)


def dot(a, b):
    return jnp.dot(a, b, preferred_element_type=F32)


def product_narrow(a, b):
    left = jnp.concatenate(halves(a), 1)
    right = jnp.concatenate(halves(b), 1)
    both = dot(left, jnp.concatenate([right, right], 0))
    return both[:, :DK] + both[:, DK:]


def product_wide(a, b):
    a_high, a_low = halves(a)
    b_high, b_low = halves(b)
    first = dot(jnp.concatenate([a_high, a_low], 1), jnp.concatenate([b_high, b_high], 0))
    return first + dot(a_high, b_low)


def unit_norm(field):
    return field * lax.rsqrt(jnp.sum(field * field, -1, keepdims=True) + 1e-06)


MESH = pl.DeviceIdType.MESH


def iotas():
    return (
        lax.broadcasted_iota(jnp.int32, (BLOCK, BLOCK), 0),
        lax.broadcasted_iota(jnp.int32, (BLOCK, BLOCK), 1),
    )


def scan_chunk(query, keys, values, strength, state_ref, o_ref, start):
    rows, width = query.shape
    groups = width // DK
    row, col = iotas()
    ident = (row == col).astype(F32)
    differ = row ^ col
    level = jnp.zeros((BLOCK, BLOCK), jnp.int32)
    for t in range(1, 7):
        level += (differ >= (1 << t)).astype(jnp.int32)
    level = jnp.where(row > col, level, -1)

    items = [(b, h) for b in range(rows // BLOCK) for h in range(groups)]

    def cut(field, b, h):
        return field[b * BLOCK : (b + 1) * BLOCK, h * DK : (h + 1) * DK]

    q = [unit_norm(cut(query, b, h)) for b, h in items]
    k = [unit_norm(cut(keys, b, h)) for b, h in items]
    beta = [strength[b * BLOCK : (b + 1) * BLOCK, h : h + 1] for b, h in items]
    k_turned = [a.T for a in k]
    grams = [product_narrow(jnp.concatenate([a, c], 0), t) for a, c, t in zip(k, q, k_turned)]
    below = [e * g[:BLOCK] for e, g in zip(beta, grams)]
    scores = [jnp.where(row >= col, g[BLOCK:], 0.0) for g in grams]
    inverse = [ident - jnp.where(level == 0, n, 0.0) for n in below]
    for t in range(1, 7):
        inner = [product_narrow(jnp.where(level == t, n, 0.0), x) for n, x in zip(below, inverse)]
        inverse = [x - product_narrow(x, y) for x, y in zip(inverse, inner)]
    uw = [
        product_wide(x, e * jnp.concatenate([cut(values, b, h), a], 1))
        for x, e, a, (b, h) in zip(inverse, beta, k, items)
    ]
    effect = [product_wide(jnp.concatenate([t, s], 0), m) for t, s, m in zip(k_turned, scores, uw)]
    zero = jnp.zeros((BLOCK, DK), F32)
    state = [state_ref[h] for h in range(groups)]
    for (b, h), g, a in zip(items, effect, q):
        step = jnp.concatenate([ident - g[:BLOCK, DK:], a - g[BLOCK:, DK:]], 0)
        after = product_wide(step, state[h])
        state[h] = after[:BLOCK] + jnp.concatenate([g[:BLOCK, :DK], zero], 1)
        o_ref[h, pl.ds(start + b * BLOCK, BLOCK), :] = after[BLOCK:] + jnp.concatenate(
            [g[BLOCK:, :DK], zero], 1
        )
    for h in range(groups):
        state_ref[h] = state[h]


def layer_kernel(
    x_hbm, wq_hbm, wk_hbm, wv_hbm, wo_hbm, b_hbm, gain_hbm, out_ref,
    x_ref, b_ref, gain_ref, w_ref, wo_ref, others, end_ref, o_ref,
    sibling_end, totals, row_in, row_out, start_out, start_in, starts, parcels, got,
    w_sem, l_sem, g_send, g_recv, f_send, f_recv,
    across_send, across_recv, first_send, first_recv, second_send, second_recv,
    third_send, third_recv, fourth_send, fourth_recv,
    pair_send, pair_recv, back_send, back_recv, z_send, z_recv, x_send, x_recv,
    a_send, a_recv,
):
    group = lax.axis_index("heads")
    me = lax.axis_index("seq")
    groups = lax.axis_size("heads")
    core, z, x = me % 2, (me // 2) % 4, me // 8
    sibling = me + 1 - 2 * core
    tokens, depth = x_ref.shape
    chunks = tokens // CHUNK
    half = CHUNK // 2

    def at(x, z, core):
        return {"seq": x * 8 + z * 2 + core}

    def beside(d):
        return {"heads": (group + d) % groups}

    def remote(src, dst, send, recv, where):
        return pltpu.make_async_remote_copy(
            src_ref=src, dst_ref=dst, send_sem=send, recv_sem=recv,
            device_id=where, device_id_type=MESH,
        )

    barrier = pltpu.get_barrier_semaphore()

    def greet(where):
        pl.semaphore_signal(barrier, inc=1, device_id=where, device_id_type=MESH)

    greet({"seq": sibling})
    for d in range(1, 4):
        greet(at(x, (z + d) % 4, core))
        greet(beside(d))
        greet(at((x + d) % 4, z, core))
    loads = [
        pltpu.make_async_copy(w, w_ref.at[i], w_sem.at[i])
        for i, w in enumerate((wq_hbm, wk_hbm, wv_hbm))
    ]
    smalls = [
        pltpu.make_async_copy(x_hbm, x_ref, l_sem.at[0]),
        pltpu.make_async_copy(b_hbm, b_ref, l_sem.at[1]),
        pltpu.make_async_copy(gain_hbm, gain_ref, l_sem.at[2]),
    ]
    for load in smalls + loads:
        load.start()
    pl.semaphore_wait(barrier, 10)

    across = [
        remote(
            wo_hbm.at[x, z, core], wo_ref.at[d, x, z, core],
            across_send.at[d - 1], across_recv.at[d - 1], beside(d),
        )
        for d in (1, 3, 2)
    ]
    back = pl.ds(1, 3)

    def along(core_now, first, d):
        if (core_now == 0) == first:
            return at(x, (z + d) % 4, core)
        return at((x + d) % 4, z, core)

    def firsts(core_now):
        return [
            remote(
                wo_ref.at[back, x, z, core_now], wo_ref.at[back, x, z, core_now],
                first_send.at[d - 1], first_recv.at[d - 1], along(core_now, True, d),
            )
            for d in (1, 3, 2)
        ]

    def line(core_now, place):
        if core_now == 0:
            return wo_ref.at[back, place, :, 0]
        return wo_ref.at[back, :, place, 1]

    def seconds(core_now):
        here = line(core_now, x if core_now == 0 else z)
        return [
            remote(
                here, here, second_send.at[d // 2], second_recv.at[d // 2],
                along(core_now, False, d),
            )
            for d in (1, 3)
        ]

    def half_line(core_now, place, j):
        if core_now == 0:
            return wo_ref.at[back, place, pl.ds(2 * j, 2), 0]
        return wo_ref.at[back, pl.ds(2 * j, 2), place, 1]

    def thirds(core_now):
        place = x if core_now == 0 else z
        return [
            remote(
                half_line(core_now, (place + 3 - 2 * j) % 4, j),
                half_line(core_now, (place + 3 - 2 * j) % 4, j),
                third_send.at[j], third_recv.at[j], along(core_now, False, 1 + 2 * j),
            )
            for j in range(2)
        ]

    def fourth():
        here = wo_ref.at[back, :, :, core]
        return remote(here, here, fourth_send.at[0], fourth_recv.at[0], {"seq": sibling})

    def either(do):
        for core_now in range(2):
            @pl.when(core == core_now)
            def _():
                do(core_now)

    def begin(copies):
        for copy in copies:
            copy.start()

    def arrived(copies):
        for copy in copies:
            copy.wait_recv()

    def left(copies):
        for copy in copies:
            copy.wait_send()

    begin(across)
    own_w = [pltpu.make_async_copy(wo_hbm, wo_ref.at[0], l_sem.at[3])]
    begin(own_w)

    def direct(c, d):
        rows = pl.ds(pl.multiple_of(c * CHUNK, CHUNK), CHUNK)
        return remote(
            x_ref.at[rows], others.at[d - 1, rows], g_send.at[c, d // 2], g_recv.at[c, d // 2],
            beside(d),
        )

    def onward(c, j):
        rows = pl.ds(pl.multiple_of(c * CHUNK + j * half, half), half)
        return remote(
            others.at[2 * j, rows], others.at[1, rows], f_send.at[c, j], f_recv.at[c, j],
            beside(1 + 2 * j),
        )

    def start_direct(c):
        direct(c, 1).start()
        direct(c, 3).start()

    def start_onward(c):
        direct(c, 1).wait_recv()
        direct(c, 3).wait_recv()
        onward(c, 0).start()
        onward(c, 1).start()

    smalls[0].wait()
    start_direct(0)
    start_direct(1)
    row, col = iotas()
    ident = (row == col).astype(F32)
    zero = jnp.zeros((DK, DK), F32)
    for h in range(end_ref.shape[0]):
        end_ref[h] = jnp.concatenate([zero, ident], 1)
    arrived(across)
    either(lambda core_now: begin(firsts(core_now)))
    start_onward(0)
    start_direct(2)
    for load in loads + smalls[1:]:
        load.wait()

    def step(c, carry):
        rows = pl.ds(pl.multiple_of(c * CHUNK, CHUNK), CHUNK)

        def part(i, d):
            source = lax.rem(group + groups - d, groups)
            piece = x_ref[rows, :] if d == 0 else others[d - 1, rows, :]
            return dot(piece, w_ref[i, pl.ds(pl.multiple_of(source * depth, depth), depth), :])

        fields = [part(i, 0) + part(i, 1) + part(i, 3) for i in range(3)]
        onward(c, 0).wait_recv()
        onward(c, 1).wait_recv()
        query, keys, values = [f + part(i, 2) for i, f in enumerate(fields)]

        @pl.when(c + 1 < chunks)
        def _():
            start_onward(c + 1)

        @pl.when(c + 3 < chunks)
        def _():
            start_direct(c + 3)

        @pl.when(c == 0)
        def _():
            def go(core_now):
                arrived(firsts(core_now))
                begin(seconds(core_now))

            either(go)

        @pl.when(c == 1)
        def _():
            def go(core_now):
                arrived(seconds(core_now))
                begin(thirds(core_now))

            either(go)

        @pl.when(c == 2)
        def _():
            either(lambda core_now: arrived(thirds(core_now)))
            fourth().start()

        strength = (b_ref[:, rows].astype(F32) * (1.0 / 64.0)).T
        scan_chunk(
            query, keys, values, strength, end_ref, o_ref, pl.multiple_of(c * CHUNK, CHUNK)
        )
        return carry

    lax.fori_loop(0, chunks, step, 0)

    mine, theirs = 2 * core, 2 - 2 * core

    def after(second, first):
        return product_wide(second[:, DK:], first) + jnp.concatenate([second[:, :DK], zero], 1)

    pairs = [
        remote(
            end_ref.at[theirs + i], sibling_end.at[i], pair_send.at[i], pair_recv.at[i],
            {"seq": sibling},
        )
        for i in range(2)
    ]
    for pair in pairs:
        pair.start()

    @pl.when(x == 0)
    def _():
        row_in[...] = jnp.zeros_like(row_in)

    early = []
    z_copies = []
    for i in range(2):
        pairs[i].wait_recv()
        own, other = end_ref[mine + i], sibling_end[i]
        first = jnp.where(core == 0, own, other)
        second = jnp.where(core == 0, other, own)
        early.append(first)
        totals[i, z] = after(second, first)
        z_copies.append(
            [
                remote(
                    totals.at[i, z], totals.at[i, z], z_send.at[i, d // 2], z_recv.at[i, d // 2],
                    at(x, (z + d) % 4, core),
                )
                for d in (1, 3)
            ]
        )
        if i == 0:
            begin(z_copies[i])

    hops = [
        remote(
            row_out.at[i], row_in.at[i], x_send.at[i], x_recv.at[i], at((x + 1) % 4, z, core)
        )
        for i in range(2)
    ]

    def set_out(i, whole):
        @pl.when(x == 0)
        def _():
            row_out[i] = whole[:, :DK]
            hops[i].start()

    def pass_on(i, whole):
        @pl.when(jnp.logical_and(x > 0, x < 3))
        def _():
            hops[i].wait_recv()
            row_out[i] = product_narrow(whole[:, DK:], row_in[i]) + whole[:, :DK]
            hops[i].start()

        @pl.when(x == 3)
        def _():
            hops[i].wait_recv()

    def z_onward(i):
        return [
            remote(
                totals.at[i, (z + 3 - 2 * j) % 4, pl.ds(j * (DK // 2), DK // 2)],
                totals.at[i, (z + 3 - 2 * j) % 4, pl.ds(j * (DK // 2), DK // 2)],
                z_send.at[i, 2 + j], z_recv.at[i, 2 + j], at(x, (z + 1 + 2 * j) % 4, core),
            )
            for j in range(2)
        ]

    def rows_of(i):
        arrived(z_onward(i))
        low = after(totals[i, 1], totals[i, 0])
        high = after(totals[i, 3], totals[i, 2])
        return low, after(high, low)

    def both_cores(i, low):
        none = jnp.concatenate([zero, ident], 1)
        third = after(totals[i, 2], low)
        head = jnp.where(
            z == 0, none, jnp.where(z == 1, totals[i, 0], jnp.where(z == 2, low, third))
        )
        return jnp.concatenate([head, after(early[i], head)], 0)

    quarter_rows = got.shape[2]
    gain = gain_ref[...]

    def parcel(i, d):
        return remote(
            parcels.at[i, d - 1], got.at[d, i], a_send.at[i, d - 1], a_recv.at[i, d - 1],
            beside(d),
        )

    backs = [
        remote(
            start_out.at[i], start_in.at[i], back_send.at[i], back_recv.at[i], {"seq": sibling}
        )
        for i in range(2)
    ]

    def states(i, both):
        state = product_narrow(both[:, DK:], row_in[i]) + both[:, :DK]
        start_out[i] = jnp.where(core == 0, state[DK:], state[:DK])
        backs[i].start()
        starts[mine + i] = jnp.where(core == 0, state[:DK], state[DK:])

    def emit(i):
        backs[i].wait_recv()
        starts[theirs + i] = start_in[i]
        for d in (2, 1, 3, 0):
            quarter = (group + d) % groups
            rows = pl.ds(pl.multiple_of(quarter * quarter_rows, quarter_rows), quarter_rows)
            for j in range(2):
                g = i + 2 * j
                piece = o_ref[g, rows, :]
                o = piece[:, :DK] + product_narrow(piece[:, DK:], starts[g])
                scale = lax.rsqrt(jnp.mean(o * o, -1, keepdims=True) + 1e-06)
                normed = (o * scale * gain).astype(BF16)
                if d == 0:
                    got[0, i, :, j * DK : (j + 1) * DK] = normed
                else:
                    parcels[i, d - 1, :, j * DK : (j + 1) * DK] = normed
            if d > 0:
                parcel(i, d).start()

    columns = out_ref.shape[1]
    tile = columns

    def mix(i, d, first=False):
        def one(n, carry):
            lanes = pl.ds(pl.multiple_of(n * tile, tile), tile)
            w = [
                wo_ref[d, i + 2 * j, :, :, :, lanes].reshape(DK, tile)
                for j in range(2)
            ]
            part = dot(got[d, i], jnp.concatenate(w, 0))
            if first:
                out_ref[:, lanes] = part
            else:
                out_ref[:, lanes] += part
            return carry

        lax.fori_loop(0, columns // tile, one, 0)

    arrived(z_copies[0])
    begin(z_onward(0))
    begin(z_copies[1])
    low0, whole0 = rows_of(0)
    set_out(0, whole0)
    both0 = both_cores(0, low0)
    arrived(z_copies[1])
    begin(z_onward(1))
    pass_on(0, whole0)
    states(0, both0)
    low1, whole1 = rows_of(1)
    set_out(1, whole1)
    both1 = both_cores(1, low1)
    emit(0)
    pass_on(1, whole1)
    states(1, both1)
    fourth().wait_recv()
    for load in own_w:
        load.wait()
    mix(0, 0, True)
    emit(1)
    mix(1, 0)
    for i in range(2):
        for d in (1, 3, 2):
            parcel(i, d).wait_recv()
            mix(i, d)

    def sent(c, carry):
        for j in range(2):
            direct(c, 1 + 2 * j).wait_send()
            onward(c, j).wait_send()
        return carry

    lax.fori_loop(0, chunks, sent, 0)
    left(across)
    either(lambda core_now: left(firsts(core_now) + seconds(core_now) + thirds(core_now)))
    left([fourth()])
    for i in range(2):
        pairs[i].wait_send()
        backs[i].wait_send()
        left(z_copies[i] + z_onward(i))
        left([parcel(i, d) for d in (1, 3, 2)])

    @pl.when(x < 3)
    def _():
        for i in range(2):
            hops[i].wait_send()


def local(inputs, w_query, w_key, w_value, w_out, beta_code, gain):
    tokens, depth = inputs.shape
    width = w_query.shape[1]
    groups = width // DK
    shares = lax.axis_size("heads")
    shards = lax.axis_size("seq")
    rows = tokens // shares
    chunks = tokens // CHUNK
    columns = w_out.shape[1]
    w_parts = w_out.reshape(4, 4, 2, width // shards, columns)
    dma = pltpu.SemaphoreType.DMA
    anywhere = pl.BlockSpec(memory_space=pl.ANY)
    return pl.pallas_call(
        layer_kernel,
        out_shape=jax.ShapeDtypeStruct((rows, columns), F32),
        in_specs=[anywhere] * 7,
        out_specs=pl.BlockSpec(memory_space=pltpu.VMEM),
        scratch_shapes=[
            pltpu.VMEM((tokens, depth), BF16),
            pltpu.VMEM((groups, tokens), jnp.int32),
            pltpu.VMEM((1, DK), F32),
            pltpu.VMEM((3, shares * depth, width), BF16),
            pltpu.VMEM((shares, 4, 4, 2, width // shards, columns), BF16),
            pltpu.VMEM((shares - 1, tokens, depth), BF16),
            pltpu.VMEM((groups, DK, 2 * DK), F32),
            pltpu.VMEM((groups, tokens, 2 * DK), F32),
            pltpu.VMEM((2, DK, 2 * DK), F32),
            pltpu.VMEM((2, 4, DK, 2 * DK), F32),
            pltpu.VMEM((2, DK, DK), F32),
            pltpu.VMEM((2, DK, DK), F32),
            pltpu.VMEM((2, DK, DK), F32),
            pltpu.VMEM((2, DK, DK), F32),
            pltpu.VMEM((groups, DK, DK), F32),
            pltpu.VMEM((2, shares - 1, rows, width // 2), BF16),
            pltpu.VMEM((shares, 2, rows, width // 2), BF16),
            dma((3,)), dma((4,)),
            dma((chunks, 2)), dma((chunks, 2)), dma((chunks, 2)), dma((chunks, 2)),
            dma((3,)), dma((3,)), dma((3,)), dma((3,)), dma((2,)), dma((2,)),
            dma((2,)), dma((2,)), dma((1,)), dma((1,)),
            dma((2,)), dma((2,)), dma((2,)), dma((2,)), dma((2, 4)), dma((2, 4)), dma((2,)), dma((2,)),
            dma((2, 3)), dma((2, 3)),
        ],
        compiler_params=pltpu.CompilerParams(
            collective_id=0, has_side_effects=True, vmem_limit_bytes=60 * 1024 * 1024
        ),
        cost_estimate=pl.CostEstimate(flops=40 * 10**9, bytes_accessed=64 << 20, transcendentals=0),
    )(inputs, w_query, w_key, w_value, w_parts, beta_code.T, gain.reshape(1, DK))


def solution(mesh):
    in_specs = (
        P("seq", "heads"),
        P(None, "heads"),
        P(None, "heads"),
        P(None, "heads"),
        P("heads", None),
        P("seq", "heads"),
        P(),
    )
    out_specs = P(("seq", "heads"), None)
    return jax.shard_map(local, mesh=mesh, in_specs=in_specs, out_specs=out_specs, check_vma=False)
```
